32 devices in a mesh: grp: 1, lat: 32 (over z, y, x, core).
Axes of the slice: x: 2, y: 2, z: 4, core: 2. Of those that a mesh axis runs over, the one named last changes fastest.
Arguments:
- grid_field: bfloat16 [192, 1440, 128], P(('grp', 'lat')), may hold values from -6 to 6
- spectral_weight: bfloat16 [4096, 2, 128, 128], P('lat'), may hold values from -0.375 to 0.375
- weight_in: bfloat16 [128, 512], replicated, may hold values from -0.5 to 0.5
- weight_out: bfloat16 [512, 128], replicated, may hold values from -0.25 to 0.25
Outputs:
- layer_out: bfloat16 [192, 1440, 128], P(('grp', 'lat'))
The draws below stay inside these ranges and needn't reach their ends.
All inputs are finite; a program needn't handle non-finite values.
Results may differ from the reference program's by a relative error of at most 0.008.
Values may be sent and summed in bfloat16 or wider, within the bound.
A program may use at most 64 MiB of HBM per device.

```python
import math
import jax
import jax.numpy as jnp
from jax import lax

C = 128
H = 512
NLON = 1440
M1 = 64
M2 = 64
NLAT = 192
MODES = 4096


def block_levels(stream_key, extent, shards, low, top_value):
    level, own = 1.0, jax.random.fold_in(stream_key, 6)
    for position, shards_of in shards:
        heights = jnp.exp(jax.random.uniform(jax.random.fold_in(own, position), (shards_of,), jnp.float32, low / len(shards), top_value / len(shards)))
        level = level * jnp.repeat(heights, extent[position] // shards_of).reshape([-1 if axis == position else 1 for axis in range(len(extent))])
    return level


def centred(rng, extent, scale, most, pieces=(), kind=jnp.bfloat16):
    drawn = scale * jax.random.normal(rng, extent, jnp.float32)
    if pieces:
        drawn = drawn * block_levels(rng, extent, pieces, -0.22, 0.18)
    return jnp.clip(drawn, -most, most).astype(kind)


def setup_inputs(seed: int = 0, part: int = 0) -> dict:
    streams_of = jax.random.split(jax.random.key(seed), 5)
    part_keys = jax.random.split(jax.random.fold_in(streams_of[4], part), 5)
    return {
        "grid_field": centred(part_keys[0], (NLAT, NLON, C), 1.0, 6.0, ((0, 32),)),
        "spectral_weight": centred(streams_of[1], (MODES, 2, C, C), (2 * C) ** -0.5, 0.375, ((0, 32),)),
        "weight_in": centred(streams_of[2], (C, H), C ** -0.5, 0.5),
        "weight_out": centred(streams_of[3], (H, C), H ** -0.5, 0.25),
    }


def longitude_forward():
    modes_lon = jnp.arange(M2, dtype=jnp.int32)
    cells_lon = jnp.arange(NLON, dtype=jnp.int32)
    angles = (modes_lon[:, None] * cells_lon[None, :] % NLON).astype(jnp.float32) * (2.0 * math.pi / NLON)
    scaled = jnp.stack([jnp.cos(angles), -jnp.sin(angles)], 1) * (1.0 / math.sqrt(NLON))
    return scaled.reshape(2 * M2, NLON).astype(jnp.bfloat16)

def longitude_inverse():
    modes_lon = jnp.arange(M2, dtype=jnp.int32)
    cells_lon = jnp.arange(NLON, dtype=jnp.int32)
    angles = (modes_lon[:, None] * cells_lon[None, :] % NLON).astype(jnp.float32) * (2.0 * math.pi / NLON)
    scaled = jnp.stack([jnp.cos(angles), -jnp.sin(angles)], 1) * (1.0 / math.sqrt(M1 * M2))
    return scaled.reshape(2 * M2, NLON).T.astype(jnp.bfloat16)

def lat_angles(wave_numbers, lat_rows, lat_count):
    product = wave_numbers[:, None] * lat_rows[None, :] % lat_count
    return product.astype(jnp.float32) * (2.0 * math.pi / lat_count)

def wave_of(mode_lat):
    return mode_lat - M1 * (mode_lat >= M1 // 2).astype(jnp.int32)

def reference(grid_field, spectral_weight, weight_in, weight_out):
    highest = lax.Precision.HIGHEST
    forward_table = longitude_forward()
    coeffs = lax.map(lambda row_cells: jnp.dot(forward_table, row_cells, preferred_element_type=jnp.float32).astype(jnp.bfloat16), grid_field)
    coeffs = coeffs.reshape(NLAT, M2, 2, C)
    waves = wave_of(jnp.arange(M1, dtype=jnp.int32))
    angles = lat_angles(waves, jnp.arange(NLAT, dtype=jnp.int32), NLAT)
    norm_lat = 1.0 / math.sqrt(NLAT)
    cos_lat = jnp.cos(angles) * norm_lat
    sin_lat = jnp.sin(angles) * norm_lat
    real_part = coeffs[:, :, 0].astype(jnp.float32)
    imag_part = coeffs[:, :, 1].astype(jnp.float32)
    real_sum = jnp.einsum('kr,rmc->kmc', cos_lat, real_part, precision=highest) + jnp.einsum('kr,rmc->kmc', sin_lat, imag_part, precision=highest)
    imag_sum = jnp.einsum('kr,rmc->kmc', cos_lat, imag_part, precision=highest) - jnp.einsum('kr,rmc->kmc', sin_lat, real_part, precision=highest)
    spectrum = jnp.stack([real_sum, imag_sum], 2).reshape(MODES, 2, C).astype(jnp.bfloat16)
    spec_real = spectrum[:, 0].astype(jnp.float32)
    spec_imag = spectrum[:, 1].astype(jnp.float32)
    weight_real = spectral_weight[:, 0].astype(jnp.float32)
    weight_imag = spectral_weight[:, 1].astype(jnp.float32)
    out_real = jnp.einsum('fi,fio->fo', spec_real, weight_real, precision=highest) - jnp.einsum('fi,fio->fo', spec_imag, weight_imag, precision=highest)
    out_imag = jnp.einsum('fi,fio->fo', spec_real, weight_imag, precision=highest) + jnp.einsum('fi,fio->fo', spec_imag, weight_real, precision=highest)
    mixed_modes = jnp.stack([out_real, out_imag], 1).astype(jnp.bfloat16)
    modes_grid = mixed_modes.astype(jnp.float32).reshape(M1, M2, 2, C)
    cos_back = jnp.cos(angles)
    sin_back = jnp.sin(angles)
    back_real = jnp.einsum('kr,kmc->rmc', cos_back, modes_grid[:, :, 0], precision=highest) - jnp.einsum('kr,kmc->rmc', sin_back, modes_grid[:, :, 1], precision=highest)
    back_imag = jnp.einsum('kr,kmc->rmc', sin_back, modes_grid[:, :, 0], precision=highest) + jnp.einsum('kr,kmc->rmc', cos_back, modes_grid[:, :, 1], precision=highest)
    inverse = jnp.stack([back_real, back_imag], 2).reshape(NLAT, 2 * M2, C).astype(jnp.bfloat16)
    inverse_table = longitude_inverse()

    def finish(pair):
        row_cells, row_modes = pair
        spatial = jnp.dot(inverse_table, row_modes, preferred_element_type=jnp.float32)
        combined = row_cells.astype(jnp.float32) + spatial
        hidden = jax.nn.gelu(jnp.dot(combined.astype(jnp.bfloat16), weight_in, preferred_element_type=jnp.float32)).astype(jnp.bfloat16)
        return (combined + jnp.dot(hidden, weight_out, preferred_element_type=jnp.float32)).astype(jnp.bfloat16)
    return lax.map(finish, (grid_field, inverse))
```

```python
import functools
import math

import jax
import jax.numpy as jnp
import ml_dtypes
import numpy as np
from jax import lax
from jax.experimental import pallas as pl
from jax.experimental.pallas import tpu as pltpu
from jax.sharding import PartitionSpec as P

M1 = 64
M2 = 64
BF = jnp.bfloat16
MESH = pl.DeviceIdType.MESH


def np_bf16(values):
    return np.asarray(values, np.float32).astype(ml_dtypes.bfloat16)


def longitude_tables(lon_count):
    modes_lon = np.arange(M2)
    cells_lon = np.arange(lon_count)
    angles = (modes_lon[:, None] * cells_lon[None, :] % lon_count) * (2.0 * math.pi / lon_count)
    both = np.stack([np.cos(angles), -np.sin(angles)], 1).reshape(2 * M2, lon_count)
    forward = np_bf16(both / math.sqrt(lon_count))
    inverse = np_bf16((both / math.sqrt(M1 * M2)).T)
    return forward, inverse


def wave_of(mode_lat):
    return mode_lat - M1 * (mode_lat >= M1 // 2).astype(np.int32)


def latitude_tables(shards, lat_dev):
    lat_count = shards * lat_dev
    mb = M2 // shards
    waves = wave_of(np.arange(M1))
    theta = (waves[:, None] * np.arange(lat_count)[None, :] % lat_count) * (
        2.0 * math.pi / lat_count
    )
    cos, sin = np.cos(theta), np.sin(theta)
    eye = np.eye(mb)
    turn = np.stack([np.stack([cos, sin], 2), np.stack([-sin, cos], 2)], 1)
    forward = np.einsum("kprq,mn->kmprnq", turn, eye) / math.sqrt(lat_count)
    forward = forward.reshape(M1 * mb * 2, lat_count * mb * 2)
    turn = np.stack([np.stack([cos, -sin], 2), np.stack([sin, cos], 2)], 1)
    turn = np.einsum("kprq->rpkq", turn)
    inverse = np.einsum("rpkq,mn->rmpknq", turn, eye)
    inverse = inverse.reshape(lat_count * mb * 2, M1 * mb * 2)
    return np_bf16(forward), np_bf16(inverse)


def swap_table(rows):
    table = np.zeros((rows, rows))
    even = np.arange(0, rows, 2)
    table[even, even + 1] = -1.0
    table[even + 1, even] = 1.0
    return np_bf16(table)


def regroup_table(shards):
    table = np.zeros((shards * 8, shards * 8))
    for a in range(2):
        for s in range(shards):
            for q in range(4):
                table[(a * shards + s) * 4 + q, (s * 2 + a) * 4 + q] = 1.0
    return np_bf16(table)


def send_all(n, me, src, dst, send_sem, recv_sem):
    own = pltpu.make_async_copy(src.at[me], dst.at[me], recv_sem)
    own.start()

    def step(s, carry):
        dest = lax.rem(me + s, n)
        pltpu.make_async_remote_copy(
            src_ref=src.at[dest],
            dst_ref=dst.at[me],
            send_sem=send_sem,
            recv_sem=recv_sem,
            device_id={"lat": dest},
            device_id_type=MESH,
        ).start()
        return carry

    lax.fori_loop(1, n, step, 0)


def wait_recv(dst, recv_sem):
    pltpu.make_async_copy(dst, dst, recv_sem).wait()


def wait_send(n, src, send_sem):
    part = src.at[pl.ds(0, n - 1)]
    pltpu.make_async_copy(part, part, send_sem).wait()


def spectral_kernel(
    n,
    grid_hbm,
    weight_hbm,
    table_hbm,
    fwd_hbm,
    inv_hbm,
    swap_hbm,
    regroup_hbm,
    out_ref,
    grid_v,
    weight_v,
    table_v,
    fwd_v,
    inv_v,
    swap_v,
    regroup_v,
    send1,
    recv1,
    send2,
    recv2,
    send3,
    recv3,
    send4,
    recv4,
    load_sem,
    send_sem,
    recv_sem,
):
    me = lax.axis_index("lat")
    lat_dev = grid_v.shape[0]
    channels = grid_v.shape[2]
    loads = [
        pltpu.make_async_copy(a, b, load_sem.at[i])
        for i, (a, b) in enumerate(
            [
                (table_hbm, table_v),
                (grid_hbm, grid_v),
                (fwd_hbm, fwd_v),
                (swap_hbm, swap_v),
                (weight_hbm, weight_v),
                (inv_hbm, inv_v),
                (regroup_hbm, regroup_v),
            ]
        )
    ]
    for load in loads:
        load.start()
    barrier = pltpu.get_barrier_semaphore()

    def greet(s, carry):
        pl.semaphore_signal(
            barrier, inc=1, device_id={"lat": lax.rem(me + s, n)}, device_id_type=MESH
        )
        return carry

    lax.fori_loop(1, n, greet, 0)
    loads[0].wait()
    loads[1].wait()
    half = 2 * M2
    low = lax.broadcasted_iota(jnp.int32, (n // 2, 8, channels), 1) < 4
    for t in range(lat_dev // 2):
        pair = jnp.concatenate([grid_v[2 * t], grid_v[2 * t + 1]], axis=1)
        got = jnp.dot(table_v[...], pair, preferred_element_type=jnp.float32)
        shape = (n // 2, 8, channels)
        a0 = got[:half, :channels].reshape(shape)
        a1 = got[:half, channels:].reshape(shape)
        b0 = got[half:, :channels].reshape(shape)
        b1 = got[half:, channels:].reshape(shape)
        even = jnp.where(low, a0, b1)
        odd = jnp.where(low, b0, a1)
        send1[:, t] = jnp.stack([even, odd], 1).reshape(n, 8, channels).astype(BF)
    pl.semaphore_wait(barrier, n - 1)
    send_all(n, me, send1, recv1, send_sem.at[0], recv_sem.at[0])
    loads[2].wait()
    wait_recv(recv1, recv_sem.at[0])
    block = recv1[...].astype(jnp.float32).reshape(-1, channels).astype(BF)
    spectrum = jnp.dot(fwd_v[...], block, preferred_element_type=jnp.float32)
    send2[...] = spectrum.reshape(n, 8, channels).astype(BF)
    send_all(n, me, send2, recv2, send_sem.at[1], recv_sem.at[1])
    loads[3].wait()
    loads[4].wait()
    wait_recv(recv2, recv_sem.at[1])
    plain = recv2[...].astype(jnp.float32).reshape(n * 8, channels).astype(BF)
    turned = jnp.dot(swap_v[...], plain, preferred_element_type=jnp.float32).astype(BF)
    both = jnp.concatenate([plain, turned], axis=1).astype(jnp.float32)
    mb = M2 // n
    row = lax.broadcasted_iota(jnp.int32, (8, channels), 0)
    for s in range(n):
        lhs = both[8 * s : 8 * s + 8].astype(BF)
        acc = None
        for q in range(4):
            f = (q // mb) * M2 + s * mb + q % mb
            part = jnp.dot(lhs, weight_v[f], preferred_element_type=jnp.float32)
            acc = part if acc is None else jnp.where(row < 2 * q, acc, part)
        send3[s] = acc.astype(BF)
    send_all(n, me, send3, recv3, send_sem.at[2], recv_sem.at[2])
    loads[5].wait()
    loads[6].wait()
    wait_recv(recv3, recv_sem.at[2])
    block = recv3[...].astype(jnp.float32).reshape(-1, channels).astype(BF)
    back = jnp.dot(inv_v[...], block, preferred_element_type=jnp.float32)
    send4[...] = back.reshape(send4.shape).astype(BF)
    send_all(n, me, send4, recv4, send_sem.at[3], recv_sem.at[3])
    wait_recv(recv4, recv_sem.at[3])
    for t in range(lat_dev // 2):
        block = recv4[:, t].astype(jnp.float32).reshape(-1, channels).astype(BF)
        rows = jnp.dot(regroup_v[...], block, preferred_element_type=jnp.float32).astype(BF)
        out_ref[t] = jnp.concatenate([rows[:half], rows[half:]], axis=1)
    wait_send(n, send1, send_sem.at[0])
    wait_send(n, send2, send_sem.at[1])
    wait_send(n, send3, send_sem.at[2])
    wait_send(n, send4, send_sem.at[3])


def spectral(n, grid_field, spectral_weight):
    lat_dev, lon_count, channels = grid_field.shape
    forward, _ = longitude_tables(lon_count)
    swapped = forward.reshape(-1, 2, 4, lon_count)[:, ::-1].reshape(2 * M2, lon_count)
    table = np.concatenate([forward, swapped], 0)
    fwd, inv = latitude_tables(n, lat_dev)
    swap = swap_table(n * 8)
    regroup = regroup_table(n)
    weight = spectral_weight.reshape(spectral_weight.shape[0], 2 * channels, channels)
    tiles = lat_dev // 2
    operands = [
        grid_field, weight, jnp.asarray(table), jnp.asarray(fwd), jnp.asarray(inv),
        jnp.asarray(swap), jnp.asarray(regroup),
    ]
    big = pltpu.VMEM((n, tiles, 8, channels), BF)
    small = pltpu.VMEM((n, 8, channels), BF)
    return pl.pallas_call(
        functools.partial(spectral_kernel, n),
        out_shape=jax.ShapeDtypeStruct((tiles, 2 * M2, 2 * channels), BF),
        in_specs=[pl.BlockSpec(memory_space=pl.ANY)] * len(operands),
        out_specs=pl.BlockSpec(memory_space=pltpu.VMEM),
        scratch_shapes=[pltpu.VMEM(x.shape, BF) for x in operands]
        + [big, big, small, small, small, small, big, big]
        + [
            pltpu.SemaphoreType.DMA((len(operands),)),
            pltpu.SemaphoreType.DMA((4,)),
            pltpu.SemaphoreType.DMA((4,)),
        ],
        compiler_params=pltpu.CompilerParams(
            collective_id=0, has_side_effects=True, vmem_limit_bytes=40 * 1024 * 1024
        ),
    )(*operands)


GELU_IN = math.sqrt(2.0 / math.pi)


def gelu(x):
    inner = x * (x * x * (0.044715 * GELU_IN) + GELU_IN)
    half = 0.5 * x
    return half + half * jnp.tanh(inner)


def finish_kernel(sub, grid_ref, inv_ref, table_ref, win_ref, wout_ref, out_ref):
    rows, channels = grid_ref.shape[1:]
    for lo in range(0, rows, sub):
        spatial = jnp.dot(
            table_ref[lo : lo + sub], inv_ref[0], preferred_element_type=jnp.float32
        )
        for a in range(2):
            cells = grid_ref[a, lo : lo + sub].astype(jnp.float32)
            combined = cells + spatial[:, a * channels : (a + 1) * channels]
            pre = jnp.dot(
                combined.astype(BF), win_ref[...], preferred_element_type=jnp.float32
            )
            hidden = gelu(pre.astype(BF))
            result = combined + jnp.dot(
                hidden, wout_ref[...], preferred_element_type=jnp.float32
            )
            out_ref[a, lo : lo + sub] = result.astype(BF)


def finish(grid_field, inverse, weight_in, weight_out):
    lat_dev, lon_count, channels = grid_field.shape
    _, table = longitude_tables(lon_count)
    block = lon_count // 2
    sub = block // 3
    return pl.pallas_call(
        functools.partial(finish_kernel, sub),
        grid=(lon_count // block, lat_dev // 2),
        out_shape=jax.ShapeDtypeStruct(grid_field.shape, BF),
        in_specs=[
            pl.BlockSpec((2, block, channels), lambda i, t: (t, i, 0)),
            pl.BlockSpec((1, 2 * M2, 2 * channels), lambda i, t: (t, 0, 0)),
            pl.BlockSpec((block, 2 * M2), lambda i, t: (i, 0)),
            pl.BlockSpec(weight_in.shape, lambda i, t: (0, 0)),
            pl.BlockSpec(weight_out.shape, lambda i, t: (0, 0)),
        ],
        out_specs=pl.BlockSpec((2, block, channels), lambda i, t: (t, i, 0)),
        compiler_params=pltpu.CompilerParams(vmem_limit_bytes=40 * 1024 * 1024),
    )(grid_field, inverse, jnp.asarray(table), weight_in, weight_out)


def spectral_wide(n, grid_field, spectral_weight):
    highest = lax.Precision.HIGHEST
    lat_dev, lon_count, channels = grid_field.shape
    lat_count = n * lat_dev
    rows = lax.axis_index("lat") * lat_dev + jnp.arange(lat_dev, dtype=jnp.int32)
    waves = jnp.asarray(wave_of(np.arange(M1)), jnp.int32)
    angles = (waves[:, None] * rows[None, :] % lat_count).astype(jnp.float32) * (
        2.0 * math.pi / lat_count
    )
    forward = jnp.asarray(longitude_tables(lon_count)[0]).reshape(M2, 2, lon_count)
    coeffs = jnp.einsum(
        "mpn,rnc->rmpc", forward, grid_field, preferred_element_type=jnp.float32
    ).astype(BF)
    cos, sin = jnp.cos(angles), jnp.sin(angles)
    turn = jnp.stack([jnp.stack([cos, sin], -1), jnp.stack([-sin, cos], -1)], 1)
    terms = jnp.einsum(
        "kprq,rmqc->kmpc",
        turn / math.sqrt(lat_count),
        coeffs.astype(jnp.float32),
        precision=highest,
    ).reshape(M1 * M2, 2, channels)
    spectrum = lax.psum_scatter(terms, "lat", scatter_dimension=0, tiled=True).astype(BF)
    product = functools.partial(
        jnp.einsum, "fi,fio->fo", preferred_element_type=jnp.float32
    )
    re, im = spectrum[:, 0], spectrum[:, 1]
    w_re, w_im = spectral_weight[:, 0], spectral_weight[:, 1]
    mixed = jnp.stack(
        [product(re, w_re) - product(im, w_im), product(re, w_im) + product(im, w_re)], 1
    ).astype(BF)
    modes = lax.all_gather(mixed, "lat", axis=0, tiled=True)
    modes = modes.astype(jnp.float32).reshape(M1, M2, 2, channels)
    turn = jnp.stack([jnp.stack([cos, -sin], -1), jnp.stack([sin, cos], -1)], 1)
    back = jnp.einsum("kprq,kmqc->rmpc", turn, modes, precision=highest)
    back = back.reshape(lat_dev // 2, 2, 2 * M2, channels).astype(BF)
    return back.transpose(0, 2, 1, 3).reshape(lat_dev // 2, 2 * M2, 2 * channels)


def per_device(grid_field, spectral_weight, weight_in, weight_out):
    n = lax.axis_size("lat")
    blocks_fit = M2 % n == 0 and M1 % n == 0 and (M1 // n) * (M2 // n) == 4
    step = spectral if blocks_fit else spectral_wide
    inverse = step(n, grid_field, spectral_weight)
    return finish(grid_field, inverse, weight_in, weight_out)


def solution(mesh):
    in_specs = (P(("grp", "lat"), None, None), P("lat", None, None, None), P(), P())
    out_specs = P(("grp", "lat"), None, None)
    return jax.shard_map(
        per_device, mesh=mesh, in_specs=in_specs, out_specs=out_specs, check_vma=False
    )
```

```python
import functools
import math

import jax
import jax.numpy as jnp
import ml_dtypes
import numpy as np
from jax import lax
from jax.experimental import pallas as pl
from jax.experimental.pallas import tpu as pltpu
from jax.sharding import PartitionSpec as P

M1 = 64
M2 = 64
BF = jnp.bfloat16
MESH = pl.DeviceIdType.MESH


def np_bf16(values):
    return np.asarray(values, np.float32).astype(ml_dtypes.bfloat16)


def longitude_tables(lon_count):
    modes_lon = np.arange(M2)
    cells_lon = np.arange(lon_count)
    angles = (modes_lon[:, None] * cells_lon[None, :] % lon_count) * (2.0 * math.pi / lon_count)
    both = np.stack([np.cos(angles), -np.sin(angles)], 1).reshape(2 * M2, lon_count)
    forward = np_bf16(both / math.sqrt(lon_count))
    inverse = np_bf16((both / math.sqrt(M1 * M2)).T)
    return forward, inverse


def wave_of(mode_lat):
    return mode_lat - M1 * (mode_lat >= M1 // 2).astype(np.int32)


def latitude_tables(shards, lat_dev):
    lat_count = shards * lat_dev
    mb = M2 // shards
    waves = wave_of(np.arange(M1))
    theta = (waves[:, None] * np.arange(lat_count)[None, :] % lat_count) * (
        2.0 * math.pi / lat_count
    )
    cos, sin = np.cos(theta), np.sin(theta)
    eye = np.eye(mb)
    turn = np.stack([np.stack([cos, sin], 2), np.stack([-sin, cos], 2)], 1)
    forward = np.einsum("kprq,mn->kmprnq", turn, eye) / math.sqrt(lat_count)
    forward = forward.reshape(M1 * mb * 2, lat_count * mb * 2)
    turn = np.stack([np.stack([cos, -sin], 2), np.stack([sin, cos], 2)], 1)
    turn = np.einsum("kprq->rpkq", turn)
    inverse = np.einsum("rpkq,mn->rmpknq", turn, eye)
    inverse = inverse.reshape(lat_count * mb * 2, M1 * mb * 2)
    return np_bf16(forward), np_bf16(inverse)


def swap_table(rows):
    table = np.zeros((rows, rows))
    even = np.arange(0, rows, 2)
    table[even, even + 1] = -1.0
    table[even + 1, even] = 1.0
    return np_bf16(table)


def regroup_table(shards):
    table = np.zeros((shards * 8, shards * 8))
    for a in range(2):
        for s in range(shards):
            for q in range(4):
                table[(a * shards + s) * 4 + q, (s * 2 + a) * 4 + q] = 1.0
    return np_bf16(table)


def send_all(n, me, src, dst, send_sem, recv_sem):
    own = pltpu.make_async_copy(src.at[me], dst.at[me], recv_sem)
    own.start()

    def step(s, carry):
        dest = lax.rem(me + s, n)
        pltpu.make_async_remote_copy(
            src_ref=src.at[dest],
            dst_ref=dst.at[me],
            send_sem=send_sem,
            recv_sem=recv_sem,
            device_id={"lat": dest},
            device_id_type=MESH,
        ).start()
        return carry

    lax.fori_loop(1, n, step, 0)


def wait_recv(dst, recv_sem):
    pltpu.make_async_copy(dst, dst, recv_sem).wait()


def wait_send(n, src, send_sem):
    part = src.at[pl.ds(0, n - 1)]
    pltpu.make_async_copy(part, part, send_sem).wait()


def spectral_kernel(
    n,
    grid_hbm,
    weight_hbm,
    table_hbm,
    fwd_hbm,
    inv_hbm,
    swap_hbm,
    regroup_hbm,
    out_ref,
    grid_v,
    weight_v,
    table_v,
    fwd_v,
    inv_v,
    swap_v,
    regroup_v,
    send1,
    recv1,
    send2,
    recv2,
    send3,
    recv3,
    send4,
    recv4,
    load_sem,
    send_sem,
    recv_sem,
):
    me = lax.axis_index("lat")
    lat_dev = grid_v.shape[0]
    channels = grid_v.shape[2]
    loads = [
        pltpu.make_async_copy(a, b, load_sem.at[i])
        for i, (a, b) in enumerate(
            [
                (table_hbm, table_v),
                (grid_hbm, grid_v),
                (fwd_hbm, fwd_v),
                (swap_hbm, swap_v),
                (weight_hbm, weight_v),
                (inv_hbm, inv_v),
                (regroup_hbm, regroup_v),
            ]
        )
    ]
    loads[0].start()
    loads[1].start()
    barrier = pltpu.get_barrier_semaphore()

    def greet(s, carry):
        pl.semaphore_signal(
            barrier, inc=1, device_id={"lat": lax.rem(me + s, n)}, device_id_type=MESH
        )
        return carry

    lax.fori_loop(1, n, greet, 0)
    loads[0].wait()
    loads[1].wait()
    for load in loads[2:]:
        load.start()
    half = 2 * M2
    low = lax.broadcasted_iota(jnp.int32, (n // 2, 8, channels), 1) < 4
    for t in range(lat_dev // 2):
        pair = jnp.concatenate([grid_v[2 * t], grid_v[2 * t + 1]], axis=1)
        got = jnp.dot(table_v[...], pair, preferred_element_type=jnp.float32)
        shape = (n // 2, 8, channels)
        a0 = got[:half, :channels].reshape(shape)
        a1 = got[:half, channels:].reshape(shape)
        b0 = got[half:, :channels].reshape(shape)
        b1 = got[half:, channels:].reshape(shape)
        even = jnp.where(low, a0, b1)
        odd = jnp.where(low, b0, a1)
        send1[:, t] = jnp.stack([even, odd], 1).reshape(n, 8, channels).astype(BF)
    pl.semaphore_wait(barrier, n - 1)
    send_all(n, me, send1, recv1, send_sem.at[0], recv_sem.at[0])
    loads[2].wait()
    wait_recv(recv1, recv_sem.at[0])
    block = recv1[...].astype(jnp.float32).reshape(-1, channels).astype(BF)
    spectrum = jnp.dot(fwd_v[...], block, preferred_element_type=jnp.float32)
    send2[...] = spectrum.reshape(n, 8, channels).astype(BF)
    send_all(n, me, send2, recv2, send_sem.at[1], recv_sem.at[1])
    loads[3].wait()
    loads[4].wait()
    wait_recv(recv2, recv_sem.at[1])
    plain = recv2[...].astype(jnp.float32).reshape(n * 8, channels).astype(BF)
    turned = jnp.dot(swap_v[...], plain, preferred_element_type=jnp.float32).astype(BF)
    both = jnp.concatenate([plain, turned], axis=1).astype(jnp.float32)
    mb = M2 // n
    row = lax.broadcasted_iota(jnp.int32, (8, channels), 0)
    for s in range(n):
        lhs = both[8 * s : 8 * s + 8].astype(BF)
        acc = None
        for q in range(4):
            f = (q // mb) * M2 + s * mb + q % mb
            part = jnp.dot(lhs, weight_v[f], preferred_element_type=jnp.float32)
            acc = part if acc is None else jnp.where(row < 2 * q, acc, part)
        send3[s] = acc.astype(BF)
    send_all(n, me, send3, recv3, send_sem.at[2], recv_sem.at[2])
    loads[5].wait()
    loads[6].wait()
    wait_recv(recv3, recv_sem.at[2])
    block = recv3[...].astype(jnp.float32).reshape(-1, channels).astype(BF)
    back = jnp.dot(inv_v[...], block, preferred_element_type=jnp.float32)
    send4[...] = back.reshape(send4.shape).astype(BF)
    send_all(n, me, send4, recv4, send_sem.at[3], recv_sem.at[3])
    wait_recv(recv4, recv_sem.at[3])
    for t in range(lat_dev // 2):
        block = recv4[:, t].astype(jnp.float32).reshape(-1, channels).astype(BF)
        rows = jnp.dot(regroup_v[...], block, preferred_element_type=jnp.float32).astype(BF)
        out_ref[t] = jnp.concatenate([rows[:half], rows[half:]], axis=1)
    wait_send(n, send1, send_sem.at[0])
    wait_send(n, send2, send_sem.at[1])
    wait_send(n, send3, send_sem.at[2])
    wait_send(n, send4, send_sem.at[3])


def spectral(n, grid_field, spectral_weight):
    lat_dev, lon_count, channels = grid_field.shape
    forward, _ = longitude_tables(lon_count)
    swapped = forward.reshape(-1, 2, 4, lon_count)[:, ::-1].reshape(2 * M2, lon_count)
    table = np.concatenate([forward, swapped], 0)
    fwd, inv = latitude_tables(n, lat_dev)
    swap = swap_table(n * 8)
    regroup = regroup_table(n)
    weight = spectral_weight.reshape(spectral_weight.shape[0], 2 * channels, channels)
    tiles = lat_dev // 2
    operands = [
        grid_field, weight, jnp.asarray(table), jnp.asarray(fwd), jnp.asarray(inv),
        jnp.asarray(swap), jnp.asarray(regroup),
    ]
    big = pltpu.VMEM((n, tiles, 8, channels), BF)
    small = pltpu.VMEM((n, 8, channels), BF)
    return pl.pallas_call(
        functools.partial(spectral_kernel, n),
        out_shape=jax.ShapeDtypeStruct((tiles, 2 * M2, 2 * channels), BF),
        in_specs=[pl.BlockSpec(memory_space=pltpu.HBM)] * len(operands),
        out_specs=pl.BlockSpec(memory_space=pltpu.VMEM),
        scratch_shapes=[pltpu.VMEM(x.shape, BF) for x in operands]
        + [big, big, small, small, small, small, big, big]
        + [
            pltpu.SemaphoreType.DMA((len(operands),)),
            pltpu.SemaphoreType.DMA((4,)),
            pltpu.SemaphoreType.DMA((4,)),
        ],
        compiler_params=pltpu.CompilerParams(
            collective_id=0, has_side_effects=True, vmem_limit_bytes=56 * 1056 * 1056
        ),
    )(*operands)


GELU_IN = math.sqrt(2.0 / math.pi)


def gelu(x):
    inner = x * (x * x * (0.044715 * GELU_IN) + GELU_IN)
    half = 0.5 * x
    return half + half * jnp.tanh(inner)


def finish_kernel(sub, grid_ref, inv_ref, table_ref, win_ref, wout_ref, out_ref):
    rows, channels = grid_ref.shape[1:]
    for lo in range(0, rows, sub):
        spatial = jnp.dot(
            table_ref[lo : lo + sub], inv_ref[0], preferred_element_type=jnp.float32
        )
        for a in range(2):
            cells = grid_ref[a, lo : lo + sub].astype(jnp.float32)
            combined = cells + spatial[:, a * channels : (a + 1) * channels]
            pre = jnp.dot(
                combined.astype(BF), win_ref[...], preferred_element_type=jnp.float32
            )
            hidden = gelu(pre.astype(BF))
            result = combined + jnp.dot(
                hidden, wout_ref[...], preferred_element_type=jnp.float32
            )
            out_ref[a, lo : lo + sub] = result.astype(BF)


def finish(grid_field, inverse, weight_in, weight_out):
    lat_dev, lon_count, channels = grid_field.shape
    _, table = longitude_tables(lon_count)
    block = lon_count
    sub = block
    return pl.pallas_call(
        functools.partial(finish_kernel, sub),
        grid=(lon_count // block, lat_dev // 2),
        out_shape=jax.ShapeDtypeStruct(grid_field.shape, BF),
        in_specs=[
            pl.BlockSpec((2, block, channels), lambda i, t: (t, i, 0)),
            pl.BlockSpec((1, 2 * M2, 2 * channels), lambda i, t: (t, 0, 0)),
            pl.BlockSpec((block, 2 * M2), lambda i, t: (i, 0)),
            pl.BlockSpec(weight_in.shape, lambda i, t: (0, 0)),
            pl.BlockSpec(weight_out.shape, lambda i, t: (0, 0)),
        ],
        out_specs=pl.BlockSpec((2, block, channels), lambda i, t: (t, i, 0)),
        compiler_params=pltpu.CompilerParams(vmem_limit_bytes=32 * 1024 * 1024),
    )(grid_field, inverse, jnp.asarray(table), weight_in, weight_out)


def spectral_wide(n, grid_field, spectral_weight):
    highest = lax.Precision.HIGHEST
    lat_dev, lon_count, channels = grid_field.shape
    lat_count = n * lat_dev
    rows = lax.axis_index("lat") * lat_dev + jnp.arange(lat_dev, dtype=jnp.int32)
    waves = jnp.asarray(wave_of(np.arange(M1)), jnp.int32)
    angles = (waves[:, None] * rows[None, :] % lat_count).astype(jnp.float32) * (
        2.0 * math.pi / lat_count
    )
    forward = jnp.asarray(longitude_tables(lon_count)[0]).reshape(M2, 2, lon_count)
    coeffs = jnp.einsum(
        "mpn,rnc->rmpc", forward, grid_field, preferred_element_type=jnp.float32
    ).astype(BF)
    cos, sin = jnp.cos(angles), jnp.sin(angles)
    turn = jnp.stack([jnp.stack([cos, sin], -1), jnp.stack([-sin, cos], -1)], 1)
    terms = jnp.einsum(
        "kprq,rmqc->kmpc",
        turn / math.sqrt(lat_count),
        coeffs.astype(jnp.float32),
        precision=highest,
    ).reshape(M1 * M2, 2, channels)
    spectrum = lax.psum_scatter(terms, "lat", scatter_dimension=0, tiled=True).astype(BF)
    product = functools.partial(
        jnp.einsum, "fi,fio->fo", preferred_element_type=jnp.float32
    )
    re, im = spectrum[:, 0], spectrum[:, 1]
    w_re, w_im = spectral_weight[:, 0], spectral_weight[:, 1]
    mixed = jnp.stack(
        [product(re, w_re) - product(im, w_im), product(re, w_im) + product(im, w_re)], 1
    ).astype(BF)
    modes = lax.all_gather(mixed, "lat", axis=0, tiled=True)
    modes = modes.astype(jnp.float32).reshape(M1, M2, 2, channels)
    turn = jnp.stack([jnp.stack([cos, -sin], -1), jnp.stack([sin, cos], -1)], 1)
    back = jnp.einsum("kprq,kmqc->rmpc", turn, modes, precision=highest)
    back = back.reshape(lat_dev // 2, 2, 2 * M2, channels).astype(BF)
    return back.transpose(0, 2, 1, 3).reshape(lat_dev // 2, 2 * M2, 2 * channels)


def per_device(grid_field, spectral_weight, weight_in, weight_out):
    n = lax.axis_size("lat")
    blocks_fit = M2 % n == 0 and M1 % n == 0 and (M1 // n) * (M2 // n) == 4
    step = spectral if blocks_fit else spectral_wide
    inverse = step(n, grid_field, spectral_weight)
    return finish(grid_field, inverse, weight_in, weight_out)


def solution(mesh):
    in_specs = (P(("grp", "lat"), None, None), P("lat", None, None, None), P(), P())
    out_specs = P(("grp", "lat"), None, None)
    return jax.shard_map(
        per_device, mesh=mesh, in_specs=in_specs, out_specs=out_specs, check_vma=False
    )
```

```python
import functools
import math

import jax
import jax.numpy as jnp
import ml_dtypes
import numpy as np
from jax import lax
from jax.experimental import pallas as pl
from jax.experimental.pallas import tpu as pltpu
from jax.sharding import PartitionSpec as P

M1 = 64
M2 = 64
BF = jnp.bfloat16
MESH = pl.DeviceIdType.MESH


def np_bf16(values):
    return np.asarray(values, np.float32).astype(ml_dtypes.bfloat16)


def longitude_tables(lon_count):
    modes_lon = np.arange(M2)
    cells_lon = np.arange(lon_count)
    angles = (modes_lon[:, None] * cells_lon[None, :] % lon_count) * (2.0 * math.pi / lon_count)
    both = np.stack([np.cos(angles), -np.sin(angles)], 1).reshape(2 * M2, lon_count)
    forward = np_bf16(both / math.sqrt(lon_count))
    inverse = np_bf16((both / math.sqrt(M1 * M2)).T)
    return forward, inverse


def wave_of(mode_lat):
    return mode_lat - M1 * (mode_lat >= M1 // 2).astype(np.int32)


def latitude_tables(shards, lat_dev):
    lat_count = shards * lat_dev
    mb = M2 // shards
    waves = wave_of(np.arange(M1))
    theta = (waves[:, None] * np.arange(lat_count)[None, :] % lat_count) * (
        2.0 * math.pi / lat_count
    )
    cos, sin = np.cos(theta), np.sin(theta)
    eye = np.eye(mb)
    turn = np.stack([np.stack([cos, sin], 2), np.stack([-sin, cos], 2)], 1)
    forward = np.einsum("kprq,mn->kmprnq", turn, eye) / math.sqrt(lat_count)
    forward = forward.reshape(M1 * mb * 2, lat_count * mb * 2)
    turn = np.stack([np.stack([cos, -sin], 2), np.stack([sin, cos], 2)], 1)
    turn = np.einsum("kprq->rpkq", turn)
    inverse = np.einsum("rpkq,mn->rmpknq", turn, eye)
    inverse = inverse.reshape(lat_count * mb * 2, M1 * mb * 2)
    return np_bf16(forward), np_bf16(inverse)


def swap_table(rows):
    table = np.zeros((rows, rows))
    even = np.arange(0, rows, 2)
    table[even, even + 1] = -1.0
    table[even + 1, even] = 1.0
    return np_bf16(table)


def regroup_table(shards):
    table = np.zeros((shards * 8, shards * 8))
    for a in range(2):
        for s in range(shards):
            for q in range(4):
                table[(a * shards + s) * 4 + q, (s * 2 + a) * 4 + q] = 1.0
    return np_bf16(table)


def send_all(n, me, src, dst, send_sem, recv_sem):
    own = pltpu.make_async_copy(src.at[me], dst.at[me], recv_sem)
    own.start()

    def step(s, carry):
        dest = lax.rem(me + s, n)
        pltpu.make_async_remote_copy(
            src_ref=src.at[dest],
            dst_ref=dst.at[me],
            send_sem=send_sem,
            recv_sem=recv_sem,
            device_id={"lat": dest},
            device_id_type=MESH,
        ).start()
        return carry

    lax.fori_loop(1, n, step, 0)


def wait_recv(dst, recv_sem):
    pltpu.make_async_copy(dst, dst, recv_sem).wait()


def wait_send(n, src, send_sem):
    part = src.at[pl.ds(0, n - 1)]
    pltpu.make_async_copy(part, part, send_sem).wait()


def spectral_kernel(
    n,
    grid_hbm,
    weight_hbm,
    table_hbm,
    fwd_hbm,
    inv_hbm,
    swap_hbm,
    regroup_hbm,
    out_ref,
    grid_v,
    weight_v,
    table_v,
    fwd_v,
    inv_v,
    swap_v,
    regroup_v,
    send1,
    recv1,
    send2,
    recv2,
    send3,
    recv3,
    send4,
    recv4,
    load_sem,
    send_sem,
    recv_sem,
):
    me = lax.axis_index("lat")
    lat_dev = grid_v.shape[0]
    channels = grid_v.shape[2]
    loads = [
        pltpu.make_async_copy(a, b, load_sem.at[i])
        for i, (a, b) in enumerate(
            [
                (table_hbm, table_v),
                (grid_hbm, grid_v),
                (fwd_hbm, fwd_v),
                (swap_hbm, swap_v),
                (weight_hbm, weight_v),
                (inv_hbm, inv_v),
                (regroup_hbm, regroup_v),
            ]
        )
    ]
    loads[0].start()
    loads[1].start()
    barrier = pltpu.get_barrier_semaphore()

    def greet(s, carry):
        pl.semaphore_signal(
            barrier, inc=1, device_id={"lat": lax.rem(me + s, n)}, device_id_type=MESH
        )
        return carry

    lax.fori_loop(1, n, greet, 0)
    loads[0].wait()
    loads[1].wait()
    for load in loads[2:]:
        load.start()
    half = 2 * M2
    low = lax.broadcasted_iota(jnp.int32, (n // 2, 8, channels), 1) < 4
    for t in range(lat_dev // 2):
        pair = jnp.concatenate([grid_v[2 * t], grid_v[2 * t + 1]], axis=1)
        got = jnp.dot(table_v[...], pair, preferred_element_type=jnp.float32)
        shape = (n // 2, 8, channels)
        a0 = got[:half, :channels].reshape(shape)
        a1 = got[:half, channels:].reshape(shape)
        b0 = got[half:, :channels].reshape(shape)
        b1 = got[half:, channels:].reshape(shape)
        even = jnp.where(low, a0, b1)
        odd = jnp.where(low, b0, a1)
        send1[:, t] = jnp.stack([even, odd], 1).reshape(n, 8, channels).astype(BF)
    pl.semaphore_wait(barrier, n - 1)
    send_all(n, me, send1, recv1, send_sem.at[0], recv_sem.at[0])
    loads[2].wait()
    wait_recv(recv1, recv_sem.at[0])
    block = recv1[...].astype(jnp.float32).reshape(-1, channels).astype(BF)
    spectrum = jnp.dot(fwd_v[...], block, preferred_element_type=jnp.float32)
    send2[...] = spectrum.reshape(n, 8, channels).astype(BF)
    send_all(n, me, send2, recv2, send_sem.at[1], recv_sem.at[1])
    loads[3].wait()
    loads[4].wait()
    wait_recv(recv2, recv_sem.at[1])
    plain = recv2[...].astype(jnp.float32).reshape(n * 8, channels).astype(BF)
    turned = jnp.dot(swap_v[...], plain, preferred_element_type=jnp.float32).astype(BF)
    both = jnp.concatenate([plain, turned], axis=1).astype(jnp.float32)
    mb = M2 // n
    row = lax.broadcasted_iota(jnp.int32, (8, channels), 0)
    for s in range(n):
        lhs = both[8 * s : 8 * s + 8].astype(BF)
        acc = None
        for q in range(4):
            f = (q // mb) * M2 + s * mb + q % mb
            part = jnp.dot(lhs, weight_v[f], preferred_element_type=jnp.float32)
            acc = part if acc is None else jnp.where(row < 2 * q, acc, part)
        send3[s] = acc.astype(BF)
    send_all(n, me, send3, recv3, send_sem.at[2], recv_sem.at[2])
    loads[5].wait()
    loads[6].wait()
    wait_recv(recv3, recv_sem.at[2])
    block = recv3[...].astype(jnp.float32).reshape(-1, channels).astype(BF)
    back = jnp.dot(inv_v[...], block, preferred_element_type=jnp.float32)
    send4[...] = back.reshape(send4.shape).astype(BF)
    send_all(n, me, send4, recv4, send_sem.at[3], recv_sem.at[3])
    wait_recv(recv4, recv_sem.at[3])
    for t in range(lat_dev // 2):
        block = recv4[:, t].astype(jnp.float32).reshape(-1, channels).astype(BF)
        rows = jnp.dot(regroup_v[...], block, preferred_element_type=jnp.float32).astype(BF)
        out_ref[t] = jnp.concatenate([rows[:half], rows[half:]], axis=1)
    wait_send(n, send1, send_sem.at[0])
    wait_send(n, send2, send_sem.at[1])
    wait_send(n, send3, send_sem.at[2])
    wait_send(n, send4, send_sem.at[3])


def spectral(n, grid_field, spectral_weight):
    lat_dev, lon_count, channels = grid_field.shape
    forward, _ = longitude_tables(lon_count)
    swapped = forward.reshape(-1, 2, 4, lon_count)[:, ::-1].reshape(2 * M2, lon_count)
    table = np.concatenate([forward, swapped], 0)
    fwd, inv = latitude_tables(n, lat_dev)
    swap = swap_table(n * 8)
    regroup = regroup_table(n)
    weight = spectral_weight.reshape(spectral_weight.shape[0], 2 * channels, channels)
    tiles = lat_dev // 2
    operands = [
        grid_field, weight, jnp.asarray(table), jnp.asarray(fwd), jnp.asarray(inv),
        jnp.asarray(swap), jnp.asarray(regroup),
    ]
    big = pltpu.VMEM((n, tiles, 8, channels), BF)
    small = pltpu.VMEM((n, 8, channels), BF)
    return pl.pallas_call(
        functools.partial(spectral_kernel, n),
        out_shape=jax.ShapeDtypeStruct((tiles, 2 * M2, 2 * channels), BF),
        in_specs=[pl.BlockSpec(memory_space=pltpu.HBM)] * len(operands),
        out_specs=pl.BlockSpec(memory_space=pltpu.VMEM),
        scratch_shapes=[pltpu.VMEM(x.shape, BF) for x in operands]
        + [big, big, small, small, small, small, big, big]
        + [
            pltpu.SemaphoreType.DMA((len(operands),)),
            pltpu.SemaphoreType.DMA((4,)),
            pltpu.SemaphoreType.DMA((4,)),
        ],
        compiler_params=pltpu.CompilerParams(
            collective_id=0, has_side_effects=True, vmem_limit_bytes=58 * 1024 * 1024
        ),
    )(*operands)


GELU_IN = math.sqrt(2.0 / math.pi)


def gelu(x):
    inner = x * (x * x * (0.044715 * GELU_IN) + GELU_IN)
    half = 0.5 * x
    return half + half * jnp.tanh(inner)


def finish_kernel(grid_ref, inv_ref, table_ref, win_ref, wout_ref, out_hbm, held, sems):
    rows, channels = grid_ref.shape[1:]
    copies = []
    for t in range(grid_ref.shape[0] // 2):
        spatial = jnp.dot(table_ref[...], inv_ref[t], preferred_element_type=jnp.float32)
        for a in range(2):
            r = 2 * t + a
            cells = grid_ref[r].astype(jnp.float32)
            combined = cells + spatial[:, a * channels : (a + 1) * channels]
            pre = jnp.dot(
                combined.astype(BF), win_ref[...], preferred_element_type=jnp.float32
            )
            hidden = gelu(pre.astype(BF))
            result = combined + jnp.dot(
                hidden, wout_ref[...], preferred_element_type=jnp.float32
            )
            held[r] = result.astype(BF)
            copy = pltpu.make_async_copy(held.at[r], out_hbm.at[r], sems.at[r])
            copy.start()
            copies.append(copy)
    for copy in copies:
        copy.wait()


def finish(grid_field, inverse, weight_in, weight_out):
    lat_dev, lon_count, _ = grid_field.shape
    _, table = longitude_tables(lon_count)
    return pl.pallas_call(
        finish_kernel,
        out_shape=jax.ShapeDtypeStruct(grid_field.shape, BF),
        in_specs=[pl.BlockSpec(memory_space=pltpu.VMEM)] * 5,
        out_specs=pl.BlockSpec(memory_space=pltpu.HBM),
        scratch_shapes=[
            pltpu.VMEM(grid_field.shape, BF),
            pltpu.SemaphoreType.DMA((lat_dev,)),
        ],
        compiler_params=pltpu.CompilerParams(vmem_limit_bytes=32 * 1024 * 1024),
    )(grid_field, inverse, jnp.asarray(table), weight_in, weight_out)


def spectral_wide(n, grid_field, spectral_weight):
    highest = lax.Precision.HIGHEST
    lat_dev, lon_count, channels = grid_field.shape
    lat_count = n * lat_dev
    rows = lax.axis_index("lat") * lat_dev + jnp.arange(lat_dev, dtype=jnp.int32)
    waves = jnp.asarray(wave_of(np.arange(M1)), jnp.int32)
    angles = (waves[:, None] * rows[None, :] % lat_count).astype(jnp.float32) * (
        2.0 * math.pi / lat_count
    )
    forward = jnp.asarray(longitude_tables(lon_count)[0]).reshape(M2, 2, lon_count)
    coeffs = jnp.einsum(
        "mpn,rnc->rmpc", forward, grid_field, preferred_element_type=jnp.float32
    ).astype(BF)
    cos, sin = jnp.cos(angles), jnp.sin(angles)
    turn = jnp.stack([jnp.stack([cos, sin], -1), jnp.stack([-sin, cos], -1)], 1)
    terms = jnp.einsum(
        "kprq,rmqc->kmpc",
        turn / math.sqrt(lat_count),
        coeffs.astype(jnp.float32),
        precision=highest,
    ).reshape(M1 * M2, 2, channels)
    spectrum = lax.psum_scatter(terms, "lat", scatter_dimension=0, tiled=True).astype(BF)
    product = functools.partial(
        jnp.einsum, "fi,fio->fo", preferred_element_type=jnp.float32
    )
    re, im = spectrum[:, 0], spectrum[:, 1]
    w_re, w_im = spectral_weight[:, 0], spectral_weight[:, 1]
    mixed = jnp.stack(
        [product(re, w_re) - product(im, w_im), product(re, w_im) + product(im, w_re)], 1
    ).astype(BF)
    modes = lax.all_gather(mixed, "lat", axis=0, tiled=True)
    modes = modes.astype(jnp.float32).reshape(M1, M2, 2, channels)
    turn = jnp.stack([jnp.stack([cos, -sin], -1), jnp.stack([sin, cos], -1)], 1)
    back = jnp.einsum("kprq,kmqc->rmpc", turn, modes, precision=highest)
    back = back.reshape(lat_dev // 2, 2, 2 * M2, channels).astype(BF)
    return back.transpose(0, 2, 1, 3).reshape(lat_dev // 2, 2 * M2, 2 * channels)


def per_device(grid_field, spectral_weight, weight_in, weight_out):
    n = lax.axis_size("lat")
    blocks_fit = M2 % n == 0 and M1 % n == 0 and (M1 // n) * (M2 // n) == 4
    step = spectral if blocks_fit else spectral_wide
    inverse = step(n, grid_field, spectral_weight)
    return finish(grid_field, inverse, weight_in, weight_out)


def solution(mesh):
    in_specs = (P(("grp", "lat"), None, None), P("lat", None, None, None), P(), P())
    out_specs = P(("grp", "lat"), None, None)
    return jax.shard_map(
        per_device, mesh=mesh, in_specs=in_specs, out_specs=out_specs, check_vma=False
    )
```
